512 devices in a mesh: user: 16 (over y, z_hi), item: 16 (over x, z_lo), layer: 2 (over core).
Axes of the slice: x: 4, y: 4, z: 16 (z_hi: 4, z_lo: 4; z = z_hi * 4 + z_lo), core: 2. Of those that a mesh axis runs over, the one named last changes fastest.
Arguments:
- user_factors: bfloat16 [64, 131072], P(None, ('user', 'item')), may hold values from -6 to 6
- item_factors: bfloat16 [64, 16384], P(None, 'item'), may hold values from -0.75 to 0.75
- ratings: bfloat16 [65536, 128, 128], P(('user', 'item', 'layer')), may hold values from -6 to 6
- masks: int32 [65536, 16, 128], P(('user', 'item', 'layer')), may hold values from 0 to 255
- tile_rows: int32 [65536], P(('user', 'item', 'layer')), may hold values from 0 to 3
- tile_cols: int32 [65536], P(('user', 'item', 'layer')), may hold values from 0 to 7
Outputs:
- grad_users: float32 [64, 131072], P(None, ('user', 'item'))
- grad_items: float32 [64, 16384], P(None, 'item')
The draws below stay inside these ranges and needn't reach their ends.
All inputs are finite; a program needn't handle non-finite values.
Results may differ from the reference program's by a relative error of at most 0.004.
Values may be sent and summed in bfloat16 or wider, within the bound.
No kernel may reach another device: no remote copies, remote signals or barrier semaphores. Data moves between devices by JAX's collectives and lax.ppermute only.
A program may use at most 64 MiB of HBM per device.

```python
import jax
import jax.numpy as jnp
from jax import lax

R = 64
TB = 128
UB_DEV = 4
IB_DEV = 8
TPS = 8
WORDS = 16
TILE_ALL = 65536
USERS = 131072
ITEMS = 16384
N_USER = 16
N_ITEM = 16
N_LAYER = 2


def touch_ends(result, own_key, low, largest):
    index_at = [jax.random.randint(jax.random.fold_in(own_key, axis), (), 0, length) for axis, length in enumerate(result.shape)]
    longest = result.shape.index(max(result.shape))
    neighbour = index_at[:longest] + [(index_at[longest] + 1) % result.shape[longest]] + index_at[longest + 1:]
    return result.at[tuple(index_at)].set(low).at[tuple(neighbour)].set(largest)


def steps_of(stream_key, extent, shards, least, top_value):
    level = 1.0
    for axis_at, blocks in shards:
        draws = jax.random.uniform(jax.random.fold_in(jax.random.fold_in(stream_key, 6), axis_at), (blocks,), jnp.float32, least / len(shards), top_value / len(shards))
        level = level * jnp.repeat(jnp.exp(draws), extent[axis_at] // blocks).reshape((-1,) + (1,) * (len(extent) - 1 - axis_at))
    return level


def centred(rng, extent, spread, limit, cuts=(), kind=jnp.bfloat16):
    loudness = steps_of(rng, extent, cuts, -0.22, 0.18) if cuts else 1.0
    values = jax.random.normal(rng, extent, jnp.float32) * spread * loudness
    return jnp.minimum(jnp.maximum(values, -limit), limit).astype(kind)


def setup_inputs(seed: int = 0) -> dict:
    key_of = jax.random.split(jax.random.key(seed), 7)
    return {
        "user_factors": centred(key_of[0], (R, USERS), 1.0, 6.0, ((1, 256),)),
        "item_factors": centred(key_of[1], (R, ITEMS), R ** -0.5, 0.75, ((1, 16),)),
        "ratings": centred(key_of[2], (TILE_ALL, TB, TB), 1.0, 6.0, ((0, 512),)),
        "masks": touch_ends(jax.random.randint(key_of[3], (TILE_ALL, WORDS, TB), 0, 256), jax.random.fold_in(key_of[3], 1), 0, 255).astype(jnp.int32),
        "tile_rows": touch_ends(jax.random.randint(key_of[4], (TILE_ALL,), 0, UB_DEV), jax.random.fold_in(key_of[4], 1), 0, UB_DEV - 1).astype(jnp.int32),
        "tile_cols": touch_ends(jax.random.randint(key_of[5], (TILE_ALL,), 0, IB_DEV), jax.random.fold_in(key_of[5], 1), 0, IB_DEV - 1).astype(jnp.int32),
    }


LOSS_SCALE = 0.0625
DECAY = 0.1


def unpack(packed):
    tiles_here, word_count, columns = packed.shape
    bit_place = jnp.arange(8, dtype=jnp.int32)
    bit_values = jnp.bitwise_and(jnp.right_shift(packed[:, :, None, :], bit_place[None, None, :, None]), 1)
    return bit_values.reshape(tiles_here, word_count * 8, columns).astype(jnp.float32)


def reference(user_factors, item_factors, ratings, masks, tile_rows, tile_cols):
    tiles_dev = TPS * N_ITEM
    user_cube = user_factors.reshape(R, USERS // TB, TB)
    item_cube = item_factors.reshape(R, ITEMS // TB, TB)
    slot_ids = jnp.arange(tiles_dev, dtype=jnp.int32)
    highest_precision = lax.Precision.HIGHEST

    def visit(state, device):
        user_sum, item_sum = state
        start_tile = (device * tiles_dev).astype(jnp.int32)
        rating = lax.dynamic_slice_in_dim(ratings, start_tile, tiles_dev, 0).astype(jnp.float32)
        observed = unpack(lax.dynamic_slice_in_dim(masks, start_tile, tiles_dev, 0))
        row_index = lax.dynamic_slice_in_dim(tile_rows, start_tile, tiles_dev, 0)
        col_index = lax.dynamic_slice_in_dim(tile_cols, start_tile, tiles_dev, 0)
        group_id = device // N_LAYER
        user_block = (group_id * UB_DEV + row_index).astype(jnp.int32)
        item_block = ((slot_ids // TPS) * IB_DEV + col_index).astype(jnp.int32)
        user_portion = jnp.take(user_cube, user_block, axis=1).astype(jnp.float32)
        item_portion = jnp.take(item_cube, item_block, axis=1).astype(jnp.float32)
        predicted_scores = jnp.einsum('bjy,bjf->jyf', user_portion, item_portion, precision=highest_precision)
        rating_residual = (observed * (predicted_scores - rating)).astype(jnp.bfloat16)
        rating_residual = lax.optimization_barrier(rating_residual).astype(jnp.float32)
        user_increment = jnp.einsum('ydw,kyw->kyd', rating_residual, item_portion, precision=highest_precision)
        item_increment = jnp.einsum('nwp,enw->enp', rating_residual, user_portion, precision=highest_precision)
        user_sum = user_sum.at[:, user_block, :].add(user_increment)
        item_sum = item_sum.at[:, item_block, :].add(item_increment)
        return (user_sum, item_sum), None

    start_state = (jnp.zeros((R, USERS // TB, TB), jnp.float32), jnp.zeros((R, ITEMS // TB, TB), jnp.float32))
    devices_all = jnp.arange(N_USER * N_ITEM * N_LAYER, dtype=jnp.int32)
    (user_sum, item_sum), _ = lax.scan(visit, start_state, devices_all)
    grad_users = LOSS_SCALE * user_sum.reshape(R, USERS) + DECAY * user_factors.astype(jnp.float32)
    grad_items = LOSS_SCALE * item_sum.reshape(R, ITEMS) + DECAY * item_factors.astype(jnp.float32)
    return grad_users, grad_items
```

```python
import jax
import jax.numpy as jnp
from jax import lax
from jax.experimental import pallas as pl
from jax.experimental.pallas import tpu as pltpu
from jax.sharding import Mesh
from jax.sharding import PartitionSpec as P

LOSS_SCALE = 0.0625
DECAY = 0.1
TB = 128
SIDE = 4
BF16 = jnp.bfloat16
F32 = jnp.float32


def tile_kernel(
    rows_ref, cols_ref, layer_ref, user_ref, own_ref, other_ref, rating_ref, mask_ref,
    keep_ref, send_ref, user_out_ref, user_t_ref, item_acc_ref,
):
    step = pl.program_id(0)
    layer = layer_ref[0]
    per_shard = rating_ref.shape[0]
    user_blocks = user_out_ref.shape[0]
    half_blocks = own_ref.shape[1]

    @pl.when(step == 0)
    def _():
        user_out_ref[...] = jnp.zeros_like(user_out_ref)
        for b in range(user_blocks):
            block = user_ref[:, b * TB:(b + 1) * TB].astype(F32)
            user_t_ref[b] = block.T.astype(BF16)

    item_acc_ref[...] = jnp.zeros_like(item_acc_ref)
    bit = jnp.left_shift(jnp.int32(1), lax.broadcasted_iota(jnp.int32, (8, TB), 0))
    words = mask_ref.shape[1]
    increments = []
    for t in range(per_shard):
        b = rows_ref[step * per_shard + t]
        c = cols_ref[step * per_shard + t]
        place = c % half_blocks
        item = jnp.where(c // half_blocks == layer, own_ref[0, place], other_ref[0, place])
        scores = jnp.dot(user_t_ref[b], item, preferred_element_type=F32)
        difference = scores - rating_ref[t].astype(F32)
        parts = []
        for w in range(words):
            word = jnp.broadcast_to(mask_ref[t, w:w + 1, :], (8, TB))
            parts.append(jnp.where((word & bit) != 0, difference[w * 8:(w + 1) * 8], 0.0))
        residual = jnp.concatenate(parts, axis=0).astype(BF16)
        user = user_ref[:, pl.ds(pl.multiple_of(b * TB, TB), TB)]
        item_inc = jnp.dot(user, residual, preferred_element_type=F32)
        user_inc = lax.dot_general(
            item, residual, (((1,), (1,)), ((), ())), preferred_element_type=F32
        )
        increments.append((b, c, user_inc, item_inc))
    for b, c, user_inc, item_inc in increments:
        user_out_ref[b] += user_inc
        item_acc_ref[c] += item_inc
    for j in range(half_blocks):
        keep_ref[0, j] = item_acc_ref[layer * half_blocks + j].astype(BF16)
        send_ref[0, j] = item_acc_ref[(1 - layer) * half_blocks + j].astype(BF16)


def tile_terms(rows, cols, layer, user_factors, own, other, ratings, masks):
    shards, half_blocks, rank, _ = own.shape
    per_shard = ratings.shape[0] // shards
    user_blocks = user_factors.shape[1] // TB
    words = masks.shape[1]
    half = pl.BlockSpec((1, half_blocks, rank, TB), lambda i, *_: (i, 0, 0, 0))
    return pl.pallas_call(
        tile_kernel,
        grid_spec=pltpu.PrefetchScalarGridSpec(
            num_scalar_prefetch=3,
            grid=(shards,),
            in_specs=[
                pl.BlockSpec(user_factors.shape, lambda i, *_: (0, 0)),
                half,
                half,
                pl.BlockSpec((per_shard, TB, TB), lambda i, *_: (i, 0, 0)),
                pl.BlockSpec((per_shard, words, TB), lambda i, *_: (i, 0, 0)),
            ],
            out_specs=[
                half,
                half,
                pl.BlockSpec((user_blocks, rank, TB), lambda i, *_: (0, 0, 0)),
            ],
            scratch_shapes=[
                pltpu.VMEM((user_blocks, TB, rank), BF16),
                pltpu.VMEM((2 * half_blocks, rank, TB), F32),
            ],
        ),
        out_shape=[
            jax.ShapeDtypeStruct(own.shape, BF16),
            jax.ShapeDtypeStruct(own.shape, BF16),
            jax.ShapeDtypeStruct((user_blocks, rank, TB), F32),
        ],
        compiler_params=pltpu.CompilerParams(vmem_limit_bytes=32 * 1024 * 1024),
        name="tile_terms",
    )(rows, cols, layer, user_factors, own, other, ratings, masks)


def spread(block, axis):
    copies = jnp.broadcast_to(block[None], (SIDE,) + block.shape)
    return lax.all_to_all(copies, axis, 0, 0)


def body(user_factors, item_factors, ratings, masks, tile_rows, tile_cols):
    rank, shard_len = item_factors.shape
    half_blocks = shard_len // TB // 2
    layer = lax.axis_index("layer")
    swap = [(0, 1), (1, 0)]

    with jax.named_scope("gather_items"):
        mine = lax.dynamic_slice_in_dim(item_factors, layer * (shard_len // 2), shard_len // 2, 1)
        mine = mine.reshape(rank, half_blocks, TB).transpose(1, 0, 2)
        own = spread(spread(mine, "item_z"), "item_x")
        own = own.reshape(SIDE * SIDE, half_blocks, rank, TB)
        other = lax.ppermute(own, "layer", swap)

    with jax.named_scope("tiles"):
        keep, send, user_part = tile_terms(
            tile_rows, tile_cols, layer.reshape(1).astype(jnp.int32), user_factors, own, other,
            ratings, masks,
        )

    with jax.named_scope("scatter_items"):
        both = (keep.astype(F32) + lax.ppermute(send, "layer", swap).astype(F32)).astype(BF16)
        both = both.reshape(SIDE, SIDE, half_blocks, rank, TB)
        over_x = lax.all_to_all(both, "item_x", 0, 0)
        over_x = over_x.astype(F32).sum(0).astype(BF16)
        over_item = lax.all_to_all(over_x, "item_z", 0, 0).astype(F32).sum(0)

    with jax.named_scope("sum_users"):
        over_z = spread(over_item.astype(BF16), "user_z").astype(F32).sum(0)
        item_half = spread(over_z, "user_y").sum(0)

    with jax.named_scope("join_layers"):
        joined = jnp.concatenate([item_half, user_part], axis=0)
        joined = lax.all_gather(joined, "layer")
        item_total = joined[:, :half_blocks].reshape(2 * half_blocks, rank, TB)
        user_total = joined[0, half_blocks:] + joined[1, half_blocks:]
        item_total = item_total.transpose(1, 0, 2).reshape(rank, shard_len)
        user_total = user_total.transpose(1, 0, 2).reshape(user_factors.shape)
        grad_users = LOSS_SCALE * user_total + DECAY * user_factors.astype(F32)
        grad_items = LOSS_SCALE * item_total + DECAY * item_factors.astype(F32)
    return (grad_users, grad_items)


def solution(mesh):
    fine = Mesh(
        mesh.devices.reshape(SIDE, SIDE, SIDE, SIDE, 2),
        ("user_y", "user_z", "item_x", "item_z", "layer"),
    )
    users = ("user_y", "user_z")
    items = ("item_x", "item_z")
    everywhere = users + items + ("layer",)
    return jax.shard_map(
        body,
        mesh=fine,
        in_specs=(
            P(None, users + items),
            P(None, items),
            P(everywhere, None, None),
            P(everywhere, None, None),
            P(everywhere),
            P(everywhere),
        ),
        out_specs=(P(None, users + items), P(None, items)),
        check_vma=False,
    )
```

```python
import jax
import jax.numpy as jnp
from jax import lax
from jax.experimental import pallas as pl
from jax.experimental.pallas import tpu as pltpu
from jax.sharding import Mesh
from jax.sharding import PartitionSpec as P

LOSS_SCALE = 0.0625
DECAY = 0.1
TB = 128
SIDE = 4
BF16 = jnp.bfloat16
F32 = jnp.float32


def tile_kernel(
    rows_ref, cols_ref, layer_ref, user_ref, own_ref, other_ref, rating_ref, mask_ref,
    keep_ref, send_ref, user_out_ref, user_t_ref, item_acc_ref,
):
    step = pl.program_id(0)
    layer = layer_ref[0]
    per_shard = rating_ref.shape[0]
    user_blocks = user_out_ref.shape[0]
    half_blocks = own_ref.shape[1]

    @pl.when(step == 0)
    def _():
        user_out_ref[...] = jnp.zeros_like(user_out_ref)
        for b in range(user_blocks):
            block = user_ref[:, b * TB:(b + 1) * TB].astype(F32)
            user_t_ref[b] = block.T.astype(BF16)

    item_acc_ref[...] = jnp.zeros_like(item_acc_ref)
    bit = jnp.left_shift(jnp.int32(1), lax.broadcasted_iota(jnp.int32, (8, TB), 0))
    words = mask_ref.shape[1]
    increments = []
    for t in range(per_shard):
        b = rows_ref[step * per_shard + t]
        c = cols_ref[step * per_shard + t]
        place = c % half_blocks
        item = jnp.where(c // half_blocks == layer, own_ref[0, place], other_ref[0, place])
        scores = jnp.dot(user_t_ref[b], item, preferred_element_type=F32)
        difference = scores - rating_ref[t].astype(F32)
        parts = []
        for w in range(words):
            word = jnp.broadcast_to(mask_ref[t, w:w + 1, :], (8, TB))
            parts.append(jnp.where((word & bit) != 0, difference[w * 8:(w + 1) * 8], 0.0))
        residual = jnp.concatenate(parts, axis=0).astype(BF16)
        user = user_ref[:, pl.ds(pl.multiple_of(b * TB, TB), TB)]
        item_inc = jnp.dot(user, residual, preferred_element_type=F32)
        user_inc = lax.dot_general(
            item, residual, (((1,), (1,)), ((), ())), preferred_element_type=F32
        )
        increments.append((b, c, user_inc, item_inc))
    for b, c, user_inc, item_inc in increments:
        user_out_ref[b] += user_inc
        item_acc_ref[c] += item_inc
    for j in range(half_blocks):
        keep_ref[0, j] = item_acc_ref[layer * half_blocks + j].astype(BF16)
        send_ref[0, j] = item_acc_ref[(1 - layer) * half_blocks + j].astype(BF16)


def tile_terms(rows, cols, layer, user_factors, own, other, ratings, masks):
    shards, half_blocks, rank, _ = own.shape
    per_shard = ratings.shape[0] // shards
    user_blocks = user_factors.shape[1] // TB
    words = masks.shape[1]
    half = pl.BlockSpec((1, half_blocks, rank, TB), lambda i, *_: (i, 0, 0, 0))
    return pl.pallas_call(
        tile_kernel,
        grid_spec=pltpu.PrefetchScalarGridSpec(
            num_scalar_prefetch=3,
            grid=(shards,),
            in_specs=[
                pl.BlockSpec(user_factors.shape, lambda i, *_: (0, 0)),
                half,
                half,
                pl.BlockSpec((per_shard, TB, TB), lambda i, *_: (i, 0, 0)),
                pl.BlockSpec((per_shard, words, TB), lambda i, *_: (i, 0, 0)),
            ],
            out_specs=[
                half,
                half,
                pl.BlockSpec((user_blocks, rank, TB), lambda i, *_: (0, 0, 0)),
            ],
            scratch_shapes=[
                pltpu.VMEM((user_blocks, TB, rank), BF16),
                pltpu.VMEM((2 * half_blocks, rank, TB), F32),
            ],
        ),
        out_shape=[
            jax.ShapeDtypeStruct(own.shape, BF16),
            jax.ShapeDtypeStruct(own.shape, BF16),
            jax.ShapeDtypeStruct((user_blocks, rank, TB), F32),
        ],
        compiler_params=pltpu.CompilerParams(vmem_limit_bytes=32 * 1024 * 1024),
        name="tile_terms",
    )(rows, cols, layer, user_factors, own, other, ratings, masks)


def spread(block, axis):
    copies = jnp.broadcast_to(block[None], (SIDE,) + block.shape)
    return lax.all_to_all(copies, axis, 0, 0)


def body(user_factors, item_factors, ratings, masks, tile_rows, tile_cols):
    rank, shard_len = item_factors.shape
    half_blocks = shard_len // TB // 2
    layer = lax.axis_index("layer")
    swap = [(0, 1), (1, 0)]

    with jax.named_scope("gather_items"):
        mine = lax.dynamic_slice_in_dim(item_factors, layer * (shard_len // 2), shard_len // 2, 1)
        mine = mine.reshape(rank, half_blocks, TB).transpose(1, 0, 2)
        own = spread(spread(mine, "item_z"), "item_x")
        own = own.reshape(SIDE * SIDE, half_blocks, rank, TB)
        other = lax.ppermute(own, "layer", swap)

    with jax.named_scope("tiles"):
        keep, send, user_part = tile_terms(
            tile_rows, tile_cols, layer.reshape(1).astype(jnp.int32), user_factors, own, other,
            ratings, masks,
        )

    with jax.named_scope("scatter_items"):
        both = (keep.astype(F32) + lax.ppermute(send, "layer", swap).astype(F32)).astype(BF16)
        both = both.reshape(SIDE, SIDE, half_blocks, rank, TB)
        over_x = lax.all_to_all(both, "item_x", 0, 0)
        over_x = over_x.astype(F32).sum(0).astype(BF16)
        over_item = lax.all_to_all(over_x, "item_z", 0, 0).astype(F32).sum(0)

    with jax.named_scope("sum_users"):
        over_z = lax.all_gather(over_item.astype(BF16), "user_z").astype(F32).sum(0)
        item_half = lax.all_gather(over_z, "user_y").sum(0)

    with jax.named_scope("join_layers"):
        joined = jnp.concatenate([item_half, user_part], axis=0)
        joined = lax.all_gather(joined, "layer")
        item_total = joined[:, :half_blocks].reshape(2 * half_blocks, rank, TB)
        user_total = joined[0, half_blocks:] + joined[1, half_blocks:]
        item_total = item_total.transpose(1, 0, 2).reshape(rank, shard_len)
        user_total = user_total.transpose(1, 0, 2).reshape(user_factors.shape)
        grad_users = LOSS_SCALE * user_total + DECAY * user_factors.astype(F32)
        grad_items = LOSS_SCALE * item_total + DECAY * item_factors.astype(F32)
    return (grad_users, grad_items)


def solution(mesh):
    fine = Mesh(
        mesh.devices.reshape(SIDE, SIDE, SIDE, SIDE, 2),
        ("user_y", "user_z", "item_x", "item_z", "layer"),
    )
    users = ("user_y", "user_z")
    items = ("item_x", "item_z")
    everywhere = users + items + ("layer",)
    return jax.shard_map(
        body,
        mesh=fine,
        in_specs=(
            P(None, users + items),
            P(None, items),
            P(everywhere, None, None),
            P(everywhere, None, None),
            P(everywhere),
            P(everywhere),
        ),
        out_specs=(P(None, users + items), P(None, items)),
        check_vma=False,
    )
```

```python
import jax
import jax.numpy as jnp
from jax import lax
from jax.experimental import pallas as pl
from jax.experimental.pallas import tpu as pltpu
from jax.sharding import Mesh
from jax.sharding import PartitionSpec as P

LOSS_SCALE = 0.0625
DECAY = 0.1
TB = 128
SIDE = 4
BF16 = jnp.bfloat16
F32 = jnp.float32


def tile_kernel(
    rows_ref, cols_ref, layer_ref, user_ref, own_ref, other_ref, rating_ref, mask_ref,
    keep_ref, send_ref, user_out_ref, user_t_ref, user_acc_ref, item_acc_ref, residual_ref,
):
    step = pl.program_id(0)
    layer = layer_ref[0]
    tiles = rating_ref.shape[0]
    shards, half_blocks = own_ref.shape[:2]
    per_shard = tiles // shards
    user_blocks = user_out_ref.shape[0]
    words = mask_ref.shape[1]

    @pl.when(step == 0)
    def _():
        user_acc_ref[...] = jnp.zeros_like(user_acc_ref)
        for b in range(user_blocks):
            block = user_ref[:, b * TB:(b + 1) * TB].astype(F32)
            user_t_ref[b] = block.T.astype(BF16)

    item_acc_ref[...] = jnp.zeros_like(item_acc_ref)

    def place(t):
        return rows_ref[step * tiles + t], cols_ref[step * tiles + t]

    def item_of(t, c):
        at = c % half_blocks
        mine, theirs = own_ref[t // per_shard, at], other_ref[t // per_shard, at]
        return jnp.where(c // half_blocks == layer, mine, theirs)

    bit = jnp.left_shift(jnp.int32(1), lax.broadcasted_iota(jnp.int32, (8, TB), 0))
    for t in range(tiles):
        b, c = place(t)
        scores = jnp.dot(user_t_ref[b], item_of(t, c), preferred_element_type=F32)
        difference = scores - rating_ref[t].astype(F32)
        parts = []
        for w in range(words):
            word = jnp.broadcast_to(mask_ref[t, w:w + 1, :], (8, TB))
            parts.append(jnp.where((word & bit) != 0, difference[w * 8:(w + 1) * 8], 0.0))
        residual_ref[t] = jnp.concatenate(parts, axis=0).astype(BF16)

    for t in range(tiles):
        b, c = place(t)
        residual = residual_ref[t]
        user = user_ref[:, pl.ds(pl.multiple_of(b * TB, TB), TB)]
        item_acc_ref[(t // per_shard) * 2 * half_blocks + c] += jnp.dot(
            user, residual, preferred_element_type=F32
        )
        user_acc_ref[b] += lax.dot_general(
            residual, item_of(t, c), (((1,), (1,)), ((), ())), preferred_element_type=F32
        )

    for g in range(shards):
        for j in range(half_blocks):
            at = g * 2 * half_blocks + j
            keep_ref[g, j] = item_acc_ref[at + layer * half_blocks].astype(BF16)
            send_ref[g, j] = item_acc_ref[at + (1 - layer) * half_blocks].astype(BF16)

    @pl.when(step == pl.num_programs(0) - 1)
    def _():
        for b in range(user_blocks):
            user_out_ref[b] = user_acc_ref[b].T


def tile_terms(rows, cols, layer, user_factors, own, other, ratings, masks):
    shards, half_blocks, rank, _ = own.shape
    tiles = ratings.shape[0] // shards * SIDE
    user_blocks = user_factors.shape[1] // TB
    words = masks.shape[1]
    half = pl.BlockSpec((SIDE, half_blocks, rank, TB), lambda i, *_: (i, 0, 0, 0))
    return pl.pallas_call(
        tile_kernel,
        grid_spec=pltpu.PrefetchScalarGridSpec(
            num_scalar_prefetch=3,
            grid=(shards // SIDE,),
            in_specs=[
                pl.BlockSpec(user_factors.shape, lambda i, *_: (0, 0)),
                half,
                half,
                pl.BlockSpec((tiles, TB, TB), lambda i, *_: (i, 0, 0)),
                pl.BlockSpec((tiles, words, TB), lambda i, *_: (i, 0, 0)),
            ],
            out_specs=[
                half,
                half,
                pl.BlockSpec((user_blocks, rank, TB), lambda i, *_: (0, 0, 0)),
            ],
            scratch_shapes=[
                pltpu.VMEM((user_blocks, TB, rank), BF16),
                pltpu.VMEM((user_blocks, TB, rank), F32),
                pltpu.VMEM((SIDE * 2 * half_blocks, rank, TB), F32),
                pltpu.VMEM((tiles, TB, TB), BF16),
            ],
        ),
        out_shape=[
            jax.ShapeDtypeStruct(own.shape, BF16),
            jax.ShapeDtypeStruct(own.shape, BF16),
            jax.ShapeDtypeStruct((user_blocks, rank, TB), F32),
        ],
        compiler_params=pltpu.CompilerParams(vmem_limit_bytes=32 * 1024 * 1024),
        name="tile_terms",
    )(rows, cols, layer, user_factors, own, other, ratings, masks)


def spread(block, axes):
    copies = jnp.broadcast_to(block[None], (lax.axis_size(axes),) + block.shape)
    return lax.all_to_all(copies, axes, 0, 0)


def body(user_factors, item_factors, ratings, masks, tile_rows, tile_cols):
    rank, shard_len = item_factors.shape
    half_blocks = shard_len // TB // 2
    layer = lax.axis_index("layer")
    swap = [(0, 1), (1, 0)]

    with jax.named_scope("gather_items"):
        mine = lax.dynamic_slice_in_dim(
            item_factors.reshape(rank, 2 * half_blocks, TB), layer * half_blocks, half_blocks, 1
        )
        own = spread(spread(mine.transpose(1, 0, 2), "item_z"), "item_x")
        own = own.reshape(SIDE * SIDE, half_blocks, rank, TB)
        other = lax.ppermute(own, "layer", swap)

    with jax.named_scope("tiles"):
        keep, send, user_part = tile_terms(
            tile_rows, tile_cols, layer.reshape(1).astype(jnp.int32), user_factors, own, other,
            ratings, masks,
        )

    with jax.named_scope("scatter_items"):
        both = (keep.astype(F32) + lax.ppermute(send, "layer", swap).astype(F32)).astype(BF16)
        both = both.reshape(SIDE, SIDE, half_blocks, rank, TB).transpose(2, 0, 1, 3, 4)
        both = both.reshape(half_blocks * SIDE, SIDE, rank, TB)
        part = lax.all_to_all(both, ("user_y", "item_x"), 0, 0)
        part = part.astype(F32).sum(0).astype(BF16)

    with jax.named_scope("sum_along_z"):
        copies = jnp.broadcast_to(part[None], (SIDE,) + part.shape)
        copies = copies.reshape((SIDE * SIDE,) + part.shape[1:])
        part = lax.all_to_all(copies, ("user_z", "item_z"), 0, 0).astype(F32).sum(0)

    with jax.named_scope("join"):
        item_half = spread(part, "user_y")
        joined = lax.all_gather(jnp.concatenate([item_half, user_part], axis=0), "layer")
        item_total = joined[:, :half_blocks].reshape(2 * half_blocks, rank, TB)
        user_total = joined[0, half_blocks:] + joined[1, half_blocks:]
        item_total = item_total.transpose(1, 0, 2).reshape(rank, shard_len)
        user_total = user_total.transpose(1, 0, 2).reshape(user_factors.shape)
        grad_users = LOSS_SCALE * user_total + DECAY * user_factors.astype(F32)
        grad_items = LOSS_SCALE * item_total + DECAY * item_factors.astype(F32)
    return (grad_users, grad_items)


def solution(mesh):
    fine = Mesh(
        mesh.devices.reshape(SIDE, SIDE, SIDE, SIDE, 2),
        ("user_y", "user_z", "item_x", "item_z", "layer"),
    )
    users = ("user_y", "user_z")
    items = ("item_x", "item_z")
    everywhere = users + items + ("layer",)
    return jax.shard_map(
        body,
        mesh=fine,
        in_specs=(
            P(None, users + items),
            P(None, items),
            P(everywhere, None, None),
            P(everywhere, None, None),
            P(everywhere),
            P(everywhere),
        ),
        out_specs=(P(None, users + items), P(None, items)),
        check_vma=False,
    )
```

```python
import jax
import jax.numpy as jnp
from jax import lax
from jax.experimental import pallas as pl
from jax.experimental.pallas import tpu as pltpu
from jax.sharding import Mesh
from jax.sharding import PartitionSpec as P

LOSS_SCALE = 0.0625
DECAY = 0.1
TB = 128
SIDE = 4
BF16 = jnp.bfloat16
F32 = jnp.float32


def tile_place(rows_ref, cols_ref, t, tiles):
    at = pl.program_id(0) * tiles + t
    return rows_ref[at], cols_ref[at]


def item_block(own_ref, other_ref, layer, shard, c):
    half_blocks = own_ref.shape[1]
    at = c % half_blocks
    return jnp.where(c // half_blocks == layer, own_ref[shard, at], other_ref[shard, at])


def item_kernel(
    rows_ref, cols_ref, layer_ref, user_ref, own_ref, other_ref, rating_ref, mask_ref,
    keep_ref, send_ref, residual_ref, user_t_ref, item_acc_ref,
):
    layer = layer_ref[0]
    tiles, words = mask_ref.shape[:2]
    shards, half_blocks = own_ref.shape[:2]
    per_shard = tiles // shards

    @pl.when(pl.program_id(0) == 0)
    def _():
        for b in range(user_t_ref.shape[0]):
            block = user_ref[:, b * TB:(b + 1) * TB].astype(F32)
            user_t_ref[b] = block.T.astype(BF16)

    item_acc_ref[...] = jnp.zeros_like(item_acc_ref)

    bit = jnp.left_shift(jnp.int32(1), lax.broadcasted_iota(jnp.int32, (8, TB), 0))
    for t in range(tiles):
        b, c = tile_place(rows_ref, cols_ref, t, tiles)
        item = item_block(own_ref, other_ref, layer, t // per_shard, c)
        scores = jnp.dot(user_t_ref[b], item, preferred_element_type=F32)
        difference = scores - rating_ref[t].astype(F32)
        parts = []
        for w in range(words):
            word = jnp.broadcast_to(mask_ref[t, w:w + 1, :], (8, TB))
            parts.append(jnp.where((word & bit) != 0, difference[w * 8:(w + 1) * 8], 0.0))
        residual_ref[t] = jnp.concatenate(parts, axis=0).astype(BF16)

    for t in range(tiles):
        b, c = tile_place(rows_ref, cols_ref, t, tiles)
        user = user_ref[:, pl.ds(pl.multiple_of(b * TB, TB), TB)]
        item_acc_ref[(t // per_shard) * 2 * half_blocks + c] += jnp.dot(
            user, residual_ref[t], preferred_element_type=F32
        )

    for g in range(shards):
        for j in range(half_blocks):
            at = g * 2 * half_blocks + j
            keep_ref[g, j] = item_acc_ref[at + layer * half_blocks].astype(BF16)
            send_ref[g, j] = item_acc_ref[at + (1 - layer) * half_blocks].astype(BF16)


def user_kernel(
    rows_ref, cols_ref, layer_ref, own_ref, other_ref, residual_ref, user_out_ref, user_acc_ref
):
    tiles = residual_ref.shape[0]
    per_shard = tiles // own_ref.shape[0]

    @pl.when(pl.program_id(0) == 0)
    def _():
        user_acc_ref[...] = jnp.zeros_like(user_acc_ref)

    for t in range(tiles):
        b, c = tile_place(rows_ref, cols_ref, t, tiles)
        item = item_block(own_ref, other_ref, layer_ref[0], t // per_shard, c)
        user_acc_ref[b] += lax.dot_general(
            residual_ref[t], item, (((1,), (1,)), ((), ())), preferred_element_type=F32
        )

    @pl.when(pl.program_id(0) == pl.num_programs(0) - 1)
    def _():
        for b in range(user_out_ref.shape[0]):
            user_out_ref[b] = user_acc_ref[b].T


def over_shards(shape):
    return pl.BlockSpec((shape[0] // SIDE,) + shape[1:], lambda i, *_: (i,) + (0,) * (len(shape) - 1))


def whole(shape):
    return pl.BlockSpec(shape, lambda i, *_: (0,) * len(shape))


def item_terms(places, user_factors, own, other, ratings, masks):
    _, half_blocks, rank, _ = own.shape
    tiles = ratings.shape[0] // SIDE
    return pl.pallas_call(
        item_kernel,
        grid_spec=pltpu.PrefetchScalarGridSpec(
            num_scalar_prefetch=3,
            grid=(SIDE,),
            in_specs=[whole(user_factors.shape)]
            + [over_shards(x.shape) for x in (own, other, ratings, masks)],
            out_specs=[over_shards(x.shape) for x in (own, own, ratings)],
            scratch_shapes=[
                pltpu.VMEM((user_factors.shape[1] // TB, TB, rank), BF16),
                pltpu.VMEM((own.shape[0] // SIDE * 2 * half_blocks, rank, TB), F32),
            ],
        ),
        out_shape=[jax.ShapeDtypeStruct(x.shape, BF16) for x in (own, own, ratings)],
        compiler_params=pltpu.CompilerParams(vmem_limit_bytes=32 * 1024 * 1024),
        name="item_terms",
    )(*places, user_factors, own, other, ratings, masks)


def user_terms(places, own, other, residual, user_blocks):
    rank = own.shape[2]
    shape = (user_blocks, rank, TB)
    return pl.pallas_call(
        user_kernel,
        grid_spec=pltpu.PrefetchScalarGridSpec(
            num_scalar_prefetch=3,
            grid=(SIDE,),
            in_specs=[over_shards(x.shape) for x in (own, other, residual)],
            out_specs=whole(shape),
            scratch_shapes=[pltpu.VMEM((user_blocks, TB, rank), F32)],
        ),
        out_shape=jax.ShapeDtypeStruct(shape, F32),
        compiler_params=pltpu.CompilerParams(vmem_limit_bytes=32 * 1024 * 1024),
        name="user_terms",
    )(*places, own, other, residual)


def spread(block, axes):
    copies = jnp.broadcast_to(block[None], (lax.axis_size(axes),) + block.shape)
    return lax.all_to_all(copies, axes, 0, 0)


def body(user_factors, item_factors, ratings, masks, tile_rows, tile_cols):
    rank, shard_len = item_factors.shape
    half_blocks = shard_len // TB // 2
    layer = lax.axis_index("layer")
    swap = [(0, 1), (1, 0)]

    with jax.named_scope("gather_items"):
        mine = lax.dynamic_slice_in_dim(
            item_factors.reshape(rank, 2 * half_blocks, TB), layer * half_blocks, half_blocks, 1
        )
        own = spread(spread(mine.transpose(1, 0, 2), "item_z"), "item_x")
        own = own.reshape(SIDE * SIDE, half_blocks, rank, TB)
        other = lax.ppermute(own, "layer", swap)

    with jax.named_scope("tiles"):
        places = (tile_rows, tile_cols, layer.reshape(1).astype(jnp.int32))
        keep, send, residual = item_terms(places, user_factors, own, other, ratings, masks)
        user_part = user_terms(places, own, other, residual, user_factors.shape[1] // TB)

    with jax.named_scope("scatter_items"):
        received = lax.ppermute(send, "layer", swap)
        received, user_part = lax.optimization_barrier((received, user_part))
        both = (keep.astype(F32) + received.astype(F32)).astype(BF16)
        both = both.reshape(SIDE, SIDE, half_blocks, rank, TB).transpose(2, 0, 1, 3, 4)
        both = both.reshape(half_blocks * SIDE, SIDE, rank, TB)
        part = lax.all_to_all(both, ("user_y", "item_x"), 0, 0)
        part = part.astype(F32).sum(0).astype(BF16)

    with jax.named_scope("sum_along_z"):
        copies = jnp.broadcast_to(part[None], (SIDE,) + part.shape)
        copies = copies.reshape((SIDE * SIDE,) + part.shape[1:])
        part = lax.all_to_all(copies, ("user_z", "item_z"), 0, 0).astype(F32).sum(0)

    with jax.named_scope("join"):
        item_half = spread(part, "user_y")
        joined = lax.all_gather(jnp.concatenate([item_half, user_part], axis=0), "layer")
        item_total = joined[:, :half_blocks].reshape(2 * half_blocks, rank, TB)
        user_total = joined[0, half_blocks:] + joined[1, half_blocks:]
        item_total = item_total.transpose(1, 0, 2).reshape(rank, shard_len)
        user_total = user_total.transpose(1, 0, 2).reshape(user_factors.shape)
        grad_users = LOSS_SCALE * user_total + DECAY * user_factors.astype(F32)
        grad_items = LOSS_SCALE * item_total + DECAY * item_factors.astype(F32)
    return (grad_users, grad_items)


def solution(mesh):
    fine = Mesh(
        mesh.devices.reshape(SIDE, SIDE, SIDE, SIDE, 2),
        ("user_y", "user_z", "item_x", "item_z", "layer"),
    )
    users = ("user_y", "user_z")
    items = ("item_x", "item_z")
    everywhere = users + items + ("layer",)
    return jax.shard_map(
        body,
        mesh=fine,
        in_specs=(
            P(None, users + items),
            P(None, items),
            P(everywhere, None, None),
            P(everywhere, None, None),
            P(everywhere),
            P(everywhere),
        ),
        out_specs=(P(None, users + items), P(None, items)),
        check_vma=False,
    )
```

```python
import jax
import jax.numpy as jnp
from jax import lax
from jax.experimental import pallas as pl
from jax.experimental.pallas import tpu as pltpu
from jax.sharding import Mesh
from jax.sharding import PartitionSpec as P

LOSS_SCALE = 0.0625
DECAY = 0.1
TB = 128
SIDE = 4
BF16 = jnp.bfloat16
F32 = jnp.float32


def tile_place(rows_ref, cols_ref, t, tiles):
    at = pl.program_id(0) * tiles + t
    return rows_ref[at], cols_ref[at]


def item_block(own_ref, other_ref, layer, shard, c):
    half_blocks = own_ref.shape[1]
    at = c % half_blocks
    return jnp.where(c // half_blocks == layer, own_ref[shard, at], other_ref[shard, at])


def item_kernel(
    rows_ref, cols_ref, layer_ref, user_ref, user_t_ref, own_ref, other_ref, rating_ref,
    mask_ref, keep_ref, send_ref, residual_ref, item_acc_ref,
):
    layer = layer_ref[0]
    tiles, words = mask_ref.shape[:2]
    shards, half_blocks = own_ref.shape[:2]
    per_shard = tiles // shards

    item_acc_ref[...] = jnp.zeros_like(item_acc_ref)

    bit = jnp.left_shift(jnp.int32(1), lax.broadcasted_iota(jnp.int32, (8, TB), 0))
    for t in range(tiles):
        b, c = tile_place(rows_ref, cols_ref, t, tiles)
        item = item_block(own_ref, other_ref, layer, t // per_shard, c)
        scores = jnp.dot(user_t_ref[b], item, preferred_element_type=F32)
        difference = scores - rating_ref[t].astype(F32)
        parts = []
        for w in range(words):
            word = jnp.broadcast_to(mask_ref[t, w:w + 1, :], (8, TB))
            parts.append(jnp.where((word & bit) != 0, difference[w * 8:(w + 1) * 8], 0.0))
        residual_ref[t] = jnp.concatenate(parts, axis=0).astype(BF16)

    for t in range(tiles):
        b, c = tile_place(rows_ref, cols_ref, t, tiles)
        user = user_ref[:, pl.ds(pl.multiple_of(b * TB, TB), TB)]
        item_acc_ref[(t // per_shard) * 2 * half_blocks + c] += jnp.dot(
            user, residual_ref[t], preferred_element_type=F32
        )

    for g in range(shards):
        for j in range(half_blocks):
            at = g * 2 * half_blocks + j
            keep_ref[g, j] = item_acc_ref[at + layer * half_blocks].astype(BF16)
            send_ref[g, j] = item_acc_ref[at + (1 - layer) * half_blocks].astype(BF16)


def user_kernel(
    rows_ref, cols_ref, layer_ref, own_ref, other_ref, residual_ref, user_out_ref, user_acc_ref
):
    tiles = residual_ref.shape[0]
    per_shard = tiles // own_ref.shape[0]

    @pl.when(pl.program_id(0) == 0)
    def _():
        user_acc_ref[...] = jnp.zeros_like(user_acc_ref)

    for t in range(tiles):
        b, c = tile_place(rows_ref, cols_ref, t, tiles)
        item = item_block(own_ref, other_ref, layer_ref[0], t // per_shard, c)
        user_acc_ref[b] += lax.dot_general(
            residual_ref[t], item, (((1,), (1,)), ((), ())), preferred_element_type=F32
        )

    @pl.when(pl.program_id(0) == pl.num_programs(0) - 1)
    def _():
        for b in range(user_out_ref.shape[0]):
            user_out_ref[b] = user_acc_ref[b].T


def over_shards(shape):
    return pl.BlockSpec((shape[0] // SIDE,) + shape[1:], lambda i, *_: (i,) + (0,) * (len(shape) - 1))


def whole(shape):
    return pl.BlockSpec(shape, lambda i, *_: (0,) * len(shape))


def item_terms(places, user_factors, user_t, own, other, ratings, masks):
    _, half_blocks, rank, _ = own.shape
    tiles = ratings.shape[0] // SIDE
    return pl.pallas_call(
        item_kernel,
        grid_spec=pltpu.PrefetchScalarGridSpec(
            num_scalar_prefetch=3,
            grid=(SIDE,),
            in_specs=[whole(user_factors.shape), whole(user_t.shape)]
            + [over_shards(x.shape) for x in (own, other, ratings, masks)],
            out_specs=[over_shards(x.shape) for x in (own, own, ratings)],
            scratch_shapes=[
                pltpu.VMEM((own.shape[0] // SIDE * 2 * half_blocks, rank, TB), F32),
            ],
        ),
        out_shape=[jax.ShapeDtypeStruct(x.shape, BF16) for x in (own, own, ratings)],
        compiler_params=pltpu.CompilerParams(vmem_limit_bytes=16 * 1024 * 1024),
        name="item_terms",
    )(*places, user_factors, user_t, own, other, ratings, masks)


def user_terms(places, own, other, residual, user_blocks):
    rank = own.shape[2]
    shape = (user_blocks, rank, TB)
    return pl.pallas_call(
        user_kernel,
        grid_spec=pltpu.PrefetchScalarGridSpec(
            num_scalar_prefetch=3,
            grid=(SIDE,),
            in_specs=[over_shards(x.shape) for x in (own, other, residual)],
            out_specs=whole(shape),
            scratch_shapes=[pltpu.VMEM((user_blocks, TB, rank), F32)],
        ),
        out_shape=jax.ShapeDtypeStruct(shape, F32),
        compiler_params=pltpu.CompilerParams(vmem_limit_bytes=16 * 1024 * 1024),
        name="user_terms",
    )(*places, own, other, residual)


def ready_kernel(user_ref, masks_ref, user_t_ref, bits_ref):
    for b in range(user_t_ref.shape[0]):
        block = user_ref[:, b * TB:(b + 1) * TB].astype(F32)
        user_t_ref[b] = block.T.astype(BF16)
    bits_ref[...] = masks_ref[...]


def ready(user_factors, masks):
    rank, users = user_factors.shape
    return pl.pallas_call(
        ready_kernel,
        out_shape=(
            jax.ShapeDtypeStruct((users // TB, TB, rank), BF16),
            jax.ShapeDtypeStruct(masks.shape, masks.dtype),
        ),
        compiler_params=pltpu.CompilerParams(vmem_limit_bytes=8 * 1024 * 1024),
        name="ready",
    )(user_factors, masks)


def spread(block, axes):
    copies = jnp.broadcast_to(block[None], (lax.axis_size(axes),) + block.shape)
    return lax.all_to_all(copies, axes, 0, 0)


def body(user_factors, item_factors, ratings, masks, tile_rows, tile_cols):
    rank, shard_len = item_factors.shape
    half_blocks = shard_len // TB // 2
    layer = lax.axis_index("layer")
    swap = [(0, 1), (1, 0)]

    with jax.named_scope("gather_items"):
        mine = lax.dynamic_slice_in_dim(
            item_factors.reshape(rank, 2 * half_blocks, TB), layer * half_blocks, half_blocks, 1
        )
        own = spread(spread(mine.transpose(1, 0, 2), "item_z"), "item_x")
        own = own.reshape(SIDE * SIDE, half_blocks, rank, TB)
        other = lax.ppermute(own, "layer", swap)
        user_t, bits = ready(user_factors, masks)
        other, user_t, bits = lax.optimization_barrier((other, user_t, bits))

    with jax.named_scope("tiles"):
        places = (tile_rows, tile_cols, layer.reshape(1).astype(jnp.int32))
        keep, send, residual = item_terms(places, user_factors, user_t, own, other, ratings, bits)
        user_part = user_terms(places, own, other, residual, user_factors.shape[1] // TB)

    with jax.named_scope("scatter_items"):
        received = lax.ppermute(send, "layer", swap)
        received, user_part = lax.optimization_barrier((received, user_part))
        both = (keep.astype(F32) + received.astype(F32)).astype(BF16)
        both = both.reshape(SIDE, SIDE, half_blocks, rank, TB).transpose(2, 0, 1, 3, 4)
        both = both.reshape(half_blocks * SIDE, SIDE, rank, TB)
        part = lax.all_to_all(both, ("user_y", "item_x"), 0, 0)
        part = part.astype(F32).sum(0).astype(BF16)

    with jax.named_scope("sum_along_z"):
        copies = jnp.broadcast_to(part[None], (SIDE,) + part.shape)
        copies = copies.reshape((SIDE * SIDE,) + part.shape[1:])
        part = lax.all_to_all(copies, ("user_z", "item_z"), 0, 0).astype(F32).sum(0)

    with jax.named_scope("join"):
        item_half = spread(part, "user_y")
        joined = lax.all_gather(jnp.concatenate([item_half, user_part], axis=0), "layer")
        item_total = joined[:, :half_blocks].reshape(2 * half_blocks, rank, TB)
        user_total = joined[0, half_blocks:] + joined[1, half_blocks:]
        item_total = item_total.transpose(1, 0, 2).reshape(rank, shard_len)
        user_total = user_total.transpose(1, 0, 2).reshape(user_factors.shape)
        grad_users = LOSS_SCALE * user_total + DECAY * user_factors.astype(F32)
        grad_items = LOSS_SCALE * item_total + DECAY * item_factors.astype(F32)
    return (grad_users, grad_items)


def solution(mesh):
    fine = Mesh(
        mesh.devices.reshape(SIDE, SIDE, SIDE, SIDE, 2),
        ("user_y", "user_z", "item_x", "item_z", "layer"),
    )
    users = ("user_y", "user_z")
    items = ("item_x", "item_z")
    everywhere = users + items + ("layer",)
    return jax.shard_map(
        body,
        mesh=fine,
        in_specs=(
            P(None, users + items),
            P(None, items),
            P(everywhere, None, None),
            P(everywhere, None, None),
            P(everywhere),
            P(everywhere),
        ),
        out_specs=(P(None, users + items), P(None, items)),
        check_vma=False,
    )
```

```python
import jax
import jax.numpy as jnp
from jax import lax
from jax.experimental import pallas as pl
from jax.experimental.pallas import tpu as pltpu
from jax.sharding import Mesh
from jax.sharding import PartitionSpec as P

LOSS_SCALE = 0.0625
DECAY = 0.1
TB = 128
SIDE = 4
BF16 = jnp.bfloat16
F32 = jnp.float32


def tile_place(rows_ref, cols_ref, t, tiles):
    at = pl.program_id(0) * tiles + t
    return rows_ref[at], cols_ref[at]


def item_block(own_ref, other_ref, layer, shard, c):
    half_blocks = own_ref.shape[1]
    side = (c >= half_blocks).astype(jnp.int32)
    at = c - half_blocks * side
    return jnp.where(side == layer, own_ref[shard, at], other_ref[shard, at])


def item_kernel(
    rows_ref, cols_ref, layer_ref, user_ref, user_t_ref, own_ref, other_ref, rating_ref,
    mask_ref, keep_ref, send_ref, residual_ref, item_acc_ref,
):
    layer = layer_ref[0]
    tiles, words = mask_ref.shape[:2]
    shards, half_blocks = own_ref.shape[:2]
    per_shard = tiles // shards

    item_acc_ref[...] = jnp.zeros_like(item_acc_ref)

    bit = jnp.left_shift(jnp.int32(1), lax.broadcasted_iota(jnp.int32, (8, TB), 0))
    for t in range(tiles):
        b, c = tile_place(rows_ref, cols_ref, t, tiles)
        item = item_block(own_ref, other_ref, layer, t // per_shard, c)
        scores = jnp.dot(user_t_ref[b], item, preferred_element_type=F32)
        difference = scores - rating_ref[t].astype(F32)
        parts = []
        for w in range(words):
            word = jnp.broadcast_to(mask_ref[t, w:w + 1, :], (8, TB))
            parts.append(jnp.where((word & bit) != 0, difference[w * 8:(w + 1) * 8], 0.0))
        residual_ref[t] = jnp.concatenate(parts, axis=0).astype(BF16)

    for t in range(tiles):
        b, c = tile_place(rows_ref, cols_ref, t, tiles)
        user = user_ref[:, pl.ds(pl.multiple_of(b * TB, TB), TB)]
        item_acc_ref[(t // per_shard) * 2 * half_blocks + c] += jnp.dot(
            user, residual_ref[t], preferred_element_type=F32
        )

    for g in range(shards):
        for j in range(half_blocks):
            at = g * 2 * half_blocks + j
            keep_ref[g, j] = item_acc_ref[at + layer * half_blocks].astype(BF16)
            send_ref[g, j] = item_acc_ref[at + (1 - layer) * half_blocks].astype(BF16)


def user_kernel(
    rows_ref, cols_ref, layer_ref, own_ref, other_ref, residual_ref, user_out_ref, user_acc_ref
):
    tiles = residual_ref.shape[0]
    per_shard = tiles // own_ref.shape[0]

    @pl.when(pl.program_id(0) == 0)
    def _():
        user_acc_ref[...] = jnp.zeros_like(user_acc_ref)

    for t in range(tiles):
        b, c = tile_place(rows_ref, cols_ref, t, tiles)
        item = item_block(own_ref, other_ref, layer_ref[0], t // per_shard, c)
        user_acc_ref[b] += lax.dot_general(
            residual_ref[t], item, (((1,), (1,)), ((), ())), preferred_element_type=F32
        )

    @pl.when(pl.program_id(0) == pl.num_programs(0) - 1)
    def _():
        for b in range(user_out_ref.shape[0]):
            user_out_ref[b] = user_acc_ref[b].T


def over_shards(shape):
    return pl.BlockSpec((shape[0] // SIDE,) + shape[1:], lambda i, *_: (i,) + (0,) * (len(shape) - 1))


def whole(shape):
    return pl.BlockSpec(shape, lambda i, *_: (0,) * len(shape))


def item_terms(places, user_factors, user_t, own, other, ratings, masks):
    _, half_blocks, rank, _ = own.shape
    tiles = ratings.shape[0] // SIDE
    return pl.pallas_call(
        item_kernel,
        grid_spec=pltpu.PrefetchScalarGridSpec(
            num_scalar_prefetch=3,
            grid=(SIDE,),
            in_specs=[whole(user_factors.shape), whole(user_t.shape)]
            + [over_shards(x.shape) for x in (own, other, ratings, masks)],
            out_specs=[over_shards(x.shape) for x in (own, own, ratings)],
            scratch_shapes=[
                pltpu.VMEM((own.shape[0] // SIDE * 2 * half_blocks, rank, TB), F32),
            ],
        ),
        out_shape=[jax.ShapeDtypeStruct(x.shape, BF16) for x in (own, own, ratings)],
        compiler_params=pltpu.CompilerParams(vmem_limit_bytes=16 * 1024 * 1024),
        name="item_terms",
    )(*places, user_factors, user_t, own, other, ratings, masks)


def user_terms(places, own, other, residual, user_blocks):
    rank = own.shape[2]
    shape = (user_blocks, rank, TB)
    return pl.pallas_call(
        user_kernel,
        grid_spec=pltpu.PrefetchScalarGridSpec(
            num_scalar_prefetch=3,
            grid=(SIDE,),
            in_specs=[over_shards(x.shape) for x in (own, other, residual)],
            out_specs=whole(shape),
            scratch_shapes=[pltpu.VMEM((user_blocks, TB, rank), F32)],
        ),
        out_shape=jax.ShapeDtypeStruct(shape, F32),
        compiler_params=pltpu.CompilerParams(vmem_limit_bytes=16 * 1024 * 1024),
        name="user_terms",
    )(*places, own, other, residual)


def ready_kernel(user_ref, masks_ref, user_t_ref, bits_ref):
    for b in range(user_t_ref.shape[0]):
        block = user_ref[:, b * TB:(b + 1) * TB].astype(F32)
        user_t_ref[b] = block.T.astype(BF16)
    bits_ref[...] = masks_ref[...]


def ready(user_factors, masks):
    rank, users = user_factors.shape
    return pl.pallas_call(
        ready_kernel,
        out_shape=(
            jax.ShapeDtypeStruct((users // TB, TB, rank), BF16),
            jax.ShapeDtypeStruct(masks.shape, masks.dtype),
        ),
        compiler_params=pltpu.CompilerParams(vmem_limit_bytes=8 * 1024 * 1024),
        name="ready",
    )(user_factors, masks)


def spread(block, axes):
    copies = jnp.broadcast_to(block[None], (lax.axis_size(axes),) + block.shape)
    return lax.all_to_all(copies, axes, 0, 0)


def body(user_factors, item_factors, ratings, masks, tile_rows, tile_cols):
    rank, shard_len = item_factors.shape
    half_blocks = shard_len // TB // 2
    layer = lax.axis_index("layer")
    swap = [(0, 1), (1, 0)]

    with jax.named_scope("gather_items"):
        mine = lax.dynamic_slice_in_dim(
            item_factors.reshape(rank, 2 * half_blocks, TB), layer * half_blocks, half_blocks, 1
        )
        own = spread(spread(mine.transpose(1, 0, 2), "item_z"), "item_x")
        own = own.reshape(SIDE * SIDE, half_blocks, rank, TB)
        other = lax.ppermute(own, "layer", swap)
        user_t, bits = ready(user_factors, masks)
        other, user_t, bits = lax.optimization_barrier((other, user_t, bits))

    with jax.named_scope("tiles"):
        places = (tile_rows, tile_cols, layer.reshape(1).astype(jnp.int32))
        keep, send, residual = item_terms(places, user_factors, user_t, own, other, ratings, bits)
        user_part = user_terms(places, own, other, residual, user_factors.shape[1] // TB)

    with jax.named_scope("scatter_items"):
        received = lax.ppermute(send, "layer", swap)
        received, user_part = lax.optimization_barrier((received, user_part))
        both = (keep.astype(F32) + received.astype(F32)).astype(BF16)
        both = both.reshape(SIDE, SIDE, half_blocks, rank, TB).transpose(0, 2, 1, 3, 4)
        both = both.reshape(half_blocks * SIDE, SIDE, rank, TB)
        part = lax.all_to_all(both, ("item_x", "user_y"), 0, 0)
        part = part.astype(F32).sum(0).astype(BF16)

    with jax.named_scope("sum_along_z"):
        copies = jnp.broadcast_to(part[None], (SIDE,) + part.shape)
        copies = copies.reshape((SIDE * SIDE,) + part.shape[1:])
        part = lax.all_to_all(copies, ("user_z", "item_z"), 0, 0).astype(F32).sum(0)

    with jax.named_scope("join"):
        item_half = spread(part, "user_y")
        joined = lax.all_gather(jnp.concatenate([item_half, user_part], axis=0), "layer")
        item_total = joined[:, :half_blocks].reshape(2 * half_blocks, rank, TB)
        user_total = joined[0, half_blocks:] + joined[1, half_blocks:]
        item_total = item_total.transpose(1, 0, 2).reshape(rank, shard_len)
        user_total = user_total.transpose(1, 0, 2).reshape(user_factors.shape)
        grad_users = LOSS_SCALE * user_total + DECAY * user_factors.astype(F32)
        grad_items = LOSS_SCALE * item_total + DECAY * item_factors.astype(F32)
    return (grad_users, grad_items)


def solution(mesh):
    fine = Mesh(
        mesh.devices.reshape(SIDE, SIDE, SIDE, SIDE, 2),
        ("user_y", "user_z", "item_x", "item_z", "layer"),
    )
    users = ("user_y", "user_z")
    items = ("item_x", "item_z")
    everywhere = users + items + ("layer",)
    return jax.shard_map(
        body,
        mesh=fine,
        in_specs=(
            P(None, users + items),
            P(None, items),
            P(everywhere, None, None),
            P(everywhere, None, None),
            P(everywhere),
            P(everywhere),
        ),
        out_specs=(P(None, users + items), P(None, items)),
        check_vma=False,
    )
```

```python
import jax
import jax.numpy as jnp
from jax import lax
from jax.experimental import pallas as pl
from jax.experimental.pallas import tpu as pltpu
from jax.sharding import Mesh
from jax.sharding import PartitionSpec as P

LOSS_SCALE = 0.0625
DECAY = 0.1
MARK = 64.0
TB = 128
SIDE = 4
BF16 = jnp.bfloat16
F32 = jnp.float32


def tile_place(rows_ref, cols_ref, t, tiles):
    at = pl.program_id(0) * tiles + t
    return rows_ref[at], cols_ref[at]


def item_block(own_ref, other_ref, layer, shard, c):
    half_blocks = own_ref.shape[1]
    side = (c >= half_blocks).astype(jnp.int32)
    at = c - half_blocks * side
    return jnp.where(side == layer, own_ref[shard, at], other_ref[shard, at])


def item_kernel(
    rows_ref, cols_ref, layer_ref, user_ref, user_t_ref, own_ref, other_ref, rating_ref,
    keep_ref, send_ref, residual_ref, item_acc_ref,
):
    layer = layer_ref[0]
    tiles = rating_ref.shape[0]
    shards, half_blocks = own_ref.shape[:2]
    per_shard = tiles // shards

    item_acc_ref[...] = jnp.zeros_like(item_acc_ref)

    for t in range(tiles):
        b, c = tile_place(rows_ref, cols_ref, t, tiles)
        item = item_block(own_ref, other_ref, layer, t // per_shard, c)
        scores = jnp.dot(user_t_ref[b], item, preferred_element_type=F32)
        rating = rating_ref[t].astype(F32)
        residual_ref[t] = jnp.where(rating < MARK, scores - rating, 0.0).astype(BF16)

    for t in range(tiles):
        b, c = tile_place(rows_ref, cols_ref, t, tiles)
        user = user_ref[:, pl.ds(pl.multiple_of(b * TB, TB), TB)]
        item_acc_ref[(t // per_shard) * 2 * half_blocks + c] += jnp.dot(
            user, residual_ref[t], preferred_element_type=F32
        )

    for g in range(shards):
        for j in range(half_blocks):
            at = g * 2 * half_blocks + j
            keep_ref[g, j] = item_acc_ref[at + layer * half_blocks].astype(BF16)
            send_ref[g, j] = item_acc_ref[at + (1 - layer) * half_blocks].astype(BF16)


def user_kernel(
    rows_ref, cols_ref, layer_ref, own_ref, other_ref, residual_ref, user_out_ref, user_acc_ref
):
    tiles = residual_ref.shape[0]
    per_shard = tiles // own_ref.shape[0]

    @pl.when(pl.program_id(0) == 0)
    def _():
        user_acc_ref[...] = jnp.zeros_like(user_acc_ref)

    for t in range(tiles):
        b, c = tile_place(rows_ref, cols_ref, t, tiles)
        item = item_block(own_ref, other_ref, layer_ref[0], t // per_shard, c)
        user_acc_ref[b] += lax.dot_general(
            residual_ref[t], item, (((1,), (1,)), ((), ())), preferred_element_type=F32
        )

    @pl.when(pl.program_id(0) == pl.num_programs(0) - 1)
    def _():
        for b in range(user_out_ref.shape[0]):
            user_out_ref[b] = user_acc_ref[b].T


def over_shards(shape):
    return pl.BlockSpec((shape[0] // SIDE,) + shape[1:], lambda i, *_: (i,) + (0,) * (len(shape) - 1))


def whole(shape):
    return pl.BlockSpec(shape, lambda i, *_: (0,) * len(shape))


def item_terms(places, user_factors, user_t, own, other, ratings):
    _, half_blocks, rank, _ = own.shape
    tiles = ratings.shape[0] // SIDE
    return pl.pallas_call(
        item_kernel,
        grid_spec=pltpu.PrefetchScalarGridSpec(
            num_scalar_prefetch=3,
            grid=(SIDE,),
            in_specs=[whole(user_factors.shape), whole(user_t.shape)]
            + [over_shards(x.shape) for x in (own, other, ratings)],
            out_specs=[over_shards(x.shape) for x in (own, own, ratings)],
            scratch_shapes=[
                pltpu.VMEM((own.shape[0] // SIDE * 2 * half_blocks, rank, TB), F32),
            ],
        ),
        out_shape=[jax.ShapeDtypeStruct(x.shape, BF16) for x in (own, own, ratings)],
        compiler_params=pltpu.CompilerParams(vmem_limit_bytes=16 * 1024 * 1024),
        name="item_terms",
    )(*places, user_factors, user_t, own, other, ratings)


def user_terms(places, own, other, residual, user_blocks):
    rank = own.shape[2]
    shape = (user_blocks, rank, TB)
    return pl.pallas_call(
        user_kernel,
        grid_spec=pltpu.PrefetchScalarGridSpec(
            num_scalar_prefetch=3,
            grid=(SIDE,),
            in_specs=[over_shards(x.shape) for x in (own, other, residual)],
            out_specs=whole(shape),
            scratch_shapes=[pltpu.VMEM((user_blocks, TB, rank), F32)],
        ),
        out_shape=jax.ShapeDtypeStruct(shape, F32),
        compiler_params=pltpu.CompilerParams(vmem_limit_bytes=16 * 1024 * 1024),
        name="user_terms",
    )(*places, own, other, residual)


def ready_kernel(user_ref, rating_ref, mask_ref, user_t_ref, marked_ref):
    for b in range(user_t_ref.shape[0]):
        block = user_ref[:, b * TB:(b + 1) * TB].astype(F32)
        user_t_ref[b] = block.T.astype(BF16)
    bit = jnp.left_shift(jnp.int32(1), lax.broadcasted_iota(jnp.int32, (8, TB), 0))

    def group(i, carry):
        for t in range(8):
            at = i * 8 + t
            rating = rating_ref[at].astype(F32)
            parts = []
            for w in range(mask_ref.shape[1]):
                word = jnp.broadcast_to(mask_ref[at, w:w + 1, :], (8, TB))
                parts.append(jnp.where((word & bit) != 0, rating[w * 8:(w + 1) * 8], MARK))
            marked_ref[at] = jnp.concatenate(parts, axis=0).astype(BF16)
        return carry

    lax.fori_loop(0, rating_ref.shape[0] // 8, group, 0)


def ready(user_factors, ratings, masks):
    rank, users = user_factors.shape
    return pl.pallas_call(
        ready_kernel,
        out_shape=(
            jax.ShapeDtypeStruct((users // TB, TB, rank), BF16),
            jax.ShapeDtypeStruct(ratings.shape, ratings.dtype),
        ),
        compiler_params=pltpu.CompilerParams(vmem_limit_bytes=24 * 1024 * 1024),
        name="ready",
    )(user_factors, ratings, masks)


def spread(block, axes):
    copies = jnp.broadcast_to(block[None], (lax.axis_size(axes),) + block.shape)
    return lax.all_to_all(copies, axes, 0, 0)


def body(user_factors, item_factors, ratings, masks, tile_rows, tile_cols):
    rank, shard_len = item_factors.shape
    half_blocks = shard_len // TB // 2
    layer = lax.axis_index("layer")
    swap = [(0, 1), (1, 0)]

    with jax.named_scope("gather_items"):
        mine = lax.dynamic_slice_in_dim(
            item_factors.reshape(rank, 2 * half_blocks, TB), layer * half_blocks, half_blocks, 1
        )
        own = spread(spread(mine.transpose(1, 0, 2), "item_z"), "item_x")
        own = own.reshape(SIDE * SIDE, half_blocks, rank, TB)
        other = lax.ppermute(own, "layer", swap)
        user_t, marked = ready(user_factors, ratings, masks)
        other, user_t, marked = lax.optimization_barrier((other, user_t, marked))

    with jax.named_scope("tiles"):
        places = (tile_rows, tile_cols, layer.reshape(1).astype(jnp.int32))
        keep, send, residual = item_terms(places, user_factors, user_t, own, other, marked)
        user_part = user_terms(places, own, other, residual, user_factors.shape[1] // TB)

    with jax.named_scope("scatter_items"):
        received = lax.ppermute(send, "layer", swap)
        received, user_part = lax.optimization_barrier((received, user_part))
        both = (keep.astype(F32) + received.astype(F32)).astype(BF16)
        both = both.reshape(SIDE, SIDE, half_blocks, rank, TB).transpose(0, 2, 1, 3, 4)
        both = both.reshape(half_blocks * SIDE, SIDE, rank, TB)
        part = lax.all_to_all(both, ("item_x", "user_y"), 0, 0)
        part = part.astype(F32).sum(0).astype(BF16)

    with jax.named_scope("sum_along_z"):
        copies = jnp.broadcast_to(part[None], (SIDE,) + part.shape)
        copies = copies.reshape((SIDE * SIDE,) + part.shape[1:])
        part = lax.all_to_all(copies, ("user_z", "item_z"), 0, 0).astype(F32).sum(0)

    with jax.named_scope("join"):
        item_half = spread(part, "user_y")
        joined = lax.all_gather(jnp.concatenate([item_half, user_part], axis=0), "layer")
        item_total = joined[:, :half_blocks].reshape(2 * half_blocks, rank, TB)
        user_total = joined[0, half_blocks:] + joined[1, half_blocks:]
        item_total = item_total.transpose(1, 0, 2).reshape(rank, shard_len)
        user_total = user_total.transpose(1, 0, 2).reshape(user_factors.shape)
        grad_users = LOSS_SCALE * user_total + DECAY * user_factors.astype(F32)
        grad_items = LOSS_SCALE * item_total + DECAY * item_factors.astype(F32)
    return (grad_users, grad_items)


def solution(mesh):
    fine = Mesh(
        mesh.devices.reshape(SIDE, SIDE, SIDE, SIDE, 2),
        ("user_y", "user_z", "item_x", "item_z", "layer"),
    )
    users = ("user_y", "user_z")
    items = ("item_x", "item_z")
    everywhere = users + items + ("layer",)
    return jax.shard_map(
        body,
        mesh=fine,
        in_specs=(
            P(None, users + items),
            P(None, items),
            P(everywhere, None, None),
            P(everywhere, None, None),
            P(everywhere),
            P(everywhere),
        ),
        out_specs=(P(None, users + items), P(None, items)),
        check_vma=False,
    )
```

```python
import jax
import jax.numpy as jnp
from jax import lax
from jax.experimental import pallas as pl
from jax.experimental.pallas import tpu as pltpu
from jax.sharding import Mesh
from jax.sharding import PartitionSpec as P

LOSS_SCALE = 0.0625
DECAY = 0.1
MARK = 64.0
TB = 128
SIDE = 4
BF16 = jnp.bfloat16
F32 = jnp.float32


def tile_place(rows_ref, cols_ref, t, tiles):
    at = pl.program_id(0) * tiles + t
    return rows_ref[at], cols_ref[at]


def item_block(own_ref, other_ref, layer, shard, c):
    half_blocks = own_ref.shape[1]
    side = (c >= half_blocks).astype(jnp.int32)
    at = c - half_blocks * side
    return jnp.where(side == layer, own_ref[shard, at], other_ref[shard, at])


def item_kernel(
    rows_ref, cols_ref, layer_ref, user_ref, user_t_ref, own_ref, other_ref, rating_ref,
    keep_ref, send_ref, residual_ref, item_acc_ref,
):
    layer = layer_ref[0]
    tiles = rating_ref.shape[0]
    shards, half_blocks = own_ref.shape[:2]
    per_shard = tiles // shards

    item_acc_ref[...] = jnp.zeros_like(item_acc_ref)

    for t in range(tiles):
        b, c = tile_place(rows_ref, cols_ref, t, tiles)
        item = item_block(own_ref, other_ref, layer, t // per_shard, c)
        scores = jnp.dot(user_t_ref[b], item, preferred_element_type=F32)
        rating = rating_ref[t].astype(F32)
        residual_ref[t] = jnp.where(rating < MARK, scores - rating, 0.0).astype(BF16)

    for t in range(tiles):
        b, c = tile_place(rows_ref, cols_ref, t, tiles)
        user = user_ref[:, pl.ds(pl.multiple_of(b * TB, TB), TB)]
        item_acc_ref[(t // per_shard) * 2 * half_blocks + c] += jnp.dot(
            user, residual_ref[t], preferred_element_type=F32
        )

    for g in range(shards):
        for j in range(half_blocks):
            at = g * 2 * half_blocks + j
            keep_ref[g, j] = item_acc_ref[at + layer * half_blocks].astype(BF16)
            send_ref[g, j] = item_acc_ref[at + (1 - layer) * half_blocks].astype(BF16)


def user_kernel(
    rows_ref, cols_ref, layer_ref, own_ref, other_ref, residual_ref, user_out_ref, user_acc_ref
):
    tiles = residual_ref.shape[0]
    per_shard = tiles // own_ref.shape[0]

    @pl.when(pl.program_id(0) == 0)
    def _():
        user_acc_ref[...] = jnp.zeros_like(user_acc_ref)

    for t in range(tiles):
        b, c = tile_place(rows_ref, cols_ref, t, tiles)
        item = item_block(own_ref, other_ref, layer_ref[0], t // per_shard, c)
        user_acc_ref[b] += lax.dot_general(
            residual_ref[t], item, (((1,), (1,)), ((), ())), preferred_element_type=F32
        )

    @pl.when(pl.program_id(0) == pl.num_programs(0) - 1)
    def _():
        for b in range(user_out_ref.shape[0]):
            user_out_ref[b] = user_acc_ref[b].T


def over_shards(shape):
    return pl.BlockSpec((shape[0] // SIDE,) + shape[1:], lambda i, *_: (i,) + (0,) * (len(shape) - 1))


def whole(shape):
    return pl.BlockSpec(shape, lambda i, *_: (0,) * len(shape))


def item_terms(places, user_factors, user_t, own, other, ratings):
    _, half_blocks, rank, _ = own.shape
    tiles = ratings.shape[0] // SIDE
    return pl.pallas_call(
        item_kernel,
        grid_spec=pltpu.PrefetchScalarGridSpec(
            num_scalar_prefetch=3,
            grid=(SIDE,),
            in_specs=[whole(user_factors.shape), whole(user_t.shape)]
            + [over_shards(x.shape) for x in (own, other, ratings)],
            out_specs=[over_shards(x.shape) for x in (own, own, ratings)],
            scratch_shapes=[
                pltpu.VMEM((own.shape[0] // SIDE * 2 * half_blocks, rank, TB), F32),
            ],
        ),
        out_shape=[jax.ShapeDtypeStruct(x.shape, BF16) for x in (own, own, ratings)],
        compiler_params=pltpu.CompilerParams(vmem_limit_bytes=16 * 1024 * 1024),
        name="item_terms",
    )(*places, user_factors, user_t, own, other, ratings)


def user_terms(places, own, other, residual, user_blocks):
    rank = own.shape[2]
    shape = (user_blocks, rank, TB)
    return pl.pallas_call(
        user_kernel,
        grid_spec=pltpu.PrefetchScalarGridSpec(
            num_scalar_prefetch=3,
            grid=(SIDE,),
            in_specs=[over_shards(x.shape) for x in (own, other, residual)],
            out_specs=whole(shape),
            scratch_shapes=[pltpu.VMEM((user_blocks, TB, rank), F32)],
        ),
        out_shape=jax.ShapeDtypeStruct(shape, F32),
        compiler_params=pltpu.CompilerParams(vmem_limit_bytes=16 * 1024 * 1024),
        name="user_terms",
    )(*places, own, other, residual)


def ready_kernel(user_ref, rating_ref, mask_ref, user_t_ref, marked_ref):
    for b in range(user_t_ref.shape[0]):
        block = user_ref[:, b * TB:(b + 1) * TB].astype(F32)
        user_t_ref[b] = block.T.astype(BF16)
    bit = jnp.left_shift(jnp.int32(1), lax.broadcasted_iota(jnp.int32, (8, TB), 0))

    def group(i, carry):
        for t in range(8):
            at = i * 8 + t
            rating = rating_ref[at].astype(F32)
            parts = []
            for w in range(mask_ref.shape[1]):
                word = jnp.broadcast_to(mask_ref[at, w:w + 1, :], (8, TB))
                parts.append(jnp.where((word & bit) != 0, rating[w * 8:(w + 1) * 8], MARK))
            marked_ref[at] = jnp.concatenate(parts, axis=0).astype(BF16)
        return carry

    lax.fori_loop(0, rating_ref.shape[0] // 8, group, 0)


def ready(user_factors, ratings, masks):
    rank, users = user_factors.shape
    return pl.pallas_call(
        ready_kernel,
        out_shape=(
            jax.ShapeDtypeStruct((users // TB, TB, rank), BF16),
            jax.ShapeDtypeStruct(ratings.shape, ratings.dtype),
        ),
        compiler_params=pltpu.CompilerParams(vmem_limit_bytes=24 * 1024 * 1024),
        name="ready",
    )(user_factors, ratings, masks)


def spread(block, axes):
    copies = jnp.broadcast_to(block[None], (lax.axis_size(axes),) + block.shape)
    return lax.all_to_all(copies, axes, 0, 0)


def body(user_factors, item_factors, ratings, masks, tile_rows, tile_cols):
    rank, shard_len = item_factors.shape
    half_blocks = shard_len // TB // 2
    layer = lax.axis_index("layer")
    swap = [(0, 1), (1, 0)]

    with jax.named_scope("gather_items"):
        mine = lax.dynamic_slice_in_dim(
            item_factors.reshape(rank, 2 * half_blocks, TB), layer * half_blocks, half_blocks, 1
        )
        own = spread(spread(mine.transpose(1, 0, 2), "item_z"), "item_x")
        own = own.reshape(SIDE * SIDE, half_blocks, rank, TB)
        other = lax.ppermute(own, "layer", swap)
        user_t, marked = ready(user_factors, ratings, masks)
        other, user_t, marked = lax.optimization_barrier((other, user_t, marked))

    with jax.named_scope("tiles"):
        places = (tile_rows, tile_cols, layer.reshape(1).astype(jnp.int32))
        keep, send, residual = item_terms(places, user_factors, user_t, own, other, marked)
        user_part = user_terms(places, own, other, residual, user_factors.shape[1] // TB)

    with jax.named_scope("scatter_items"):
        received = lax.ppermute(send, "layer", swap)
        received, user_part = lax.optimization_barrier((received, user_part))
        both = (keep.astype(F32) + received.astype(F32)).astype(BF16)
        both = both.reshape(SIDE, SIDE, half_blocks, rank, TB).transpose(0, 2, 1, 3, 4)
        both = both.reshape(half_blocks * SIDE, SIDE, rank, TB)
        part = lax.all_to_all(both, ("item_x", "user_y"), 0, 0)
        part = part.astype(F32).sum(0).astype(BF16)

    with jax.named_scope("sum_along_z"):
        copies = jnp.broadcast_to(part[None], (SIDE,) + part.shape)
        copies = copies.reshape((SIDE * SIDE,) + part.shape[1:])
        part = lax.all_to_all(copies, ("user_z", "item_z"), 0, 0).astype(F32).sum(0)

    with jax.named_scope("join"):
        joined = lax.all_gather(jnp.concatenate([part[None], user_part], axis=0), "layer")
        user_total = joined[0, 1:] + joined[1, 1:]
        user_total = user_total.transpose(1, 0, 2).reshape(user_factors.shape)
        grad_users = LOSS_SCALE * user_total + DECAY * user_factors.astype(F32)
        pieces, grad_users = lax.optimization_barrier((joined[:, 0], grad_users))
        item_total = spread(pieces, "user_y").transpose(2, 1, 0, 3).reshape(rank, shard_len)
        grad_items = LOSS_SCALE * item_total + DECAY * item_factors.astype(F32)
    return (grad_users, grad_items)


def solution(mesh):
    fine = Mesh(
        mesh.devices.reshape(SIDE, SIDE, SIDE, SIDE, 2),
        ("user_y", "user_z", "item_x", "item_z", "layer"),
    )
    users = ("user_y", "user_z")
    items = ("item_x", "item_z")
    everywhere = users + items + ("layer",)
    return jax.shard_map(
        body,
        mesh=fine,
        in_specs=(
            P(None, users + items),
            P(None, items),
            P(everywhere, None, None),
            P(everywhere, None, None),
            P(everywhere),
            P(everywhere),
        ),
        out_specs=(P(None, users + items), P(None, items)),
        check_vma=False,
    )
```
